256 devices in a mesh: row: 32 (over z_lo, x, core), col: 8 (over y, z_hi).
Axes of the slice: x: 4, y: 4, z: 8 (z_hi: 2, z_lo: 4; z = z_hi * 4 + z_lo), core: 2. Of those that a mesh axis runs over, the one named last changes fastest.
Arguments:
- amplitudes: bfloat16 [1536, 65536], P('row', 'col'), may hold values from -6 to 6
- integrals: bfloat16 [2048, 65536], P(None, ('col', 'row')), may hold values from -0.09375 to 0.09375
- residual_in: float32 [1536, 2048], P('row', 'col'), may hold values from -6 to 6
Outputs:
- residual_out: float32 [1536, 2048], P('row', 'col')
The draws below stay inside these ranges and needn't reach their ends.
All inputs are finite; a program needn't handle non-finite values.
Results may differ from the reference program's by a relative error of at most 0.0003.
Values may be sent and summed in bfloat16 or wider, within the bound.
A program may use at most 64 MiB of HBM per device.

```python
import jax
import jax.numpy as jnp
from jax import lax

IJ = 1536
AB = 2048
CD = 65536


def spiked(drawn, own_key, source, target, parts, factor):
    def block_of(axis_at):
        return (jnp.arange(drawn.shape[axis_at]) // (drawn.shape[axis_at] // parts)).reshape((-1,) + (1,) * (drawn.ndim - 1 - axis_at))

    first = jax.random.permutation(own_key, parts)[block_of(target)]
    far = (block_of(target) + parts // 2) % parts
    return jnp.where((block_of(source) == first) | (block_of(source) == far), factor * drawn, drawn)


def shard_levels(stream_key, shape, split, least, largest):
    def one(position, shards_of):
        heights = jax.random.uniform(jax.random.fold_in(jax.random.fold_in(stream_key, 6), position), (shards_of,), jnp.float32, least / len(split), largest / len(split))
        return jnp.repeat(jnp.exp(heights), shape[position] // shards_of).reshape((-1,) + (1,) * (len(shape) - position - 1))

    gain = one(*split[0])
    for cut in split[1:]:
        gain = gain * one(*cut)
    return gain


def noise(stream_key, extent, deviation, limit, split=(), dtype=jnp.bfloat16):
    values = deviation * jax.random.normal(stream_key, extent, jnp.float32)
    if split:
        values = values * shard_levels(stream_key, extent, split, -0.22, 0.18)
    return jnp.clip(values, -limit, limit).astype(dtype)


def noise_with(rng, dims, deviation, most, split, heavy, kind=jnp.bfloat16):
    entries = deviation * jax.random.normal(rng, dims, jnp.float32)
    if split:
        entries = entries * shard_levels(rng, dims, split, -0.22, 0.18)
    return jnp.clip(spiked(entries, jax.random.fold_in(rng, 3), *heavy), -most, most).astype(kind)


def setup_inputs(seed: int = 0) -> dict:
    seeds = jax.random.split(jax.random.key(seed), 4)
    amplitudes = noise_with(seeds[0], (IJ, CD), 1.0, 6.0, ((0, 32), (1, 8)), (1, 0, 32, 2.75))
    integrals = noise_with(seeds[1], (AB, CD), CD ** -0.5, 0.09375, ((1, 256),), (1, 0, 256, 6.0))
    residual_in = noise(seeds[2], (IJ, AB), 1.0, 6.0, ((0, 32), (1, 8)), jnp.float32)
    return dict(amplitudes=amplitudes, integrals=integrals, residual_in=residual_in)


def reference(amplitudes, integrals, residual_in):
    ladder = lax.dot_general(amplitudes.astype(jnp.float32), integrals.astype(jnp.float32), (((1,), (1,)), ((), ())), preferred_element_type=jnp.float32)
    return residual_in + ladder
```

```python
import functools

import jax
import jax.numpy as jnp
from jax import lax
from jax.experimental import pallas as pl
from jax.experimental.pallas import tpu as pltpu
from jax.sharding import PartitionSpec as P

MESH = pl.DeviceIdType.MESH
ROWS = 48
COLS = 256
UNIT = 256
DEPTH = 4 * UNIT
BLOCKS = 8
OFFSETS = (2, 1, 3, 0)
TOP = (0, 4, 3, 6)
BOTTOM = (2, 1, 5, 7)


def device(x, y, z, core):
    x, y, z = lax.rem(x + 4, 4), lax.rem(y + 4, 4), lax.rem(z + 8, 8)
    return (lax.rem(z, 4) * 8 + x * 2 + core, y * 2 + lax.div(z, 4))


def kernel(
    a_ref, b_ref, out_ref,
    a_all, b_all, part, near, far, z_first, z_ring, z_last, x_last,
    a_send, a_recv, b_local, mate_send, mate_recv, bx_send, bx_recv, fw_send, fw_recv,
    near_send, near_recv, far_send, far_recv, zf_send, zf_recv, zr_send, zr_recv, zl_send, zl_recv, xl_send, xl_recv,
):
    row, col = lax.axis_index("row"), lax.axis_index("col")
    core = lax.rem(row, 2)
    x = lax.rem(lax.div(row, 2), 4)
    z_low = lax.div(row, 8)
    y = lax.div(col, 2)
    z_high = lax.rem(col, 2)
    z = z_high * 4 + z_low
    mate = device(x, y, z, 1 - core)
    toward = 1 - 2 * core
    way = 1 - lax.rem(z_low, 2)
    sign = 1 - 2 * way

    z_lows = (z_low, z_low + 1 - 2 * lax.rem(z_low, 2), 3 - z_low, lax.rem(z_low + 2, 4))

    barrier = pltpu.get_barrier_semaphore()
    partners = [mate, device(x + 1, y, z, core), device(x - 1, y, z, core)]
    partners += [device(x, y + 1, z, core), device(x, y - 1, z, core)]
    partners += [device(x + dx, y, z + dz, core) for dx in (0, 2) for dz in (1, -1)]
    partners += [device(x + dx, y, z_high * 4 + low, core) for low in z_lows for dx in (0, 2)][1:]
    for partner in partners:
        pl.semaphore_signal(barrier, inc=1, device_id=partner, device_id_type=MESH)

    def unit(start):
        return pl.ds(pl.multiple_of(start * UNIT, UNIT), UNIT)

    def a_pieces(dx, low):
        there = lax.rem(x + dx, 4)
        block = a_all.at[z_low, pl.ds(ROWS * (dx // 2), ROWS)]
        for units, slot, length in (
            (low * 8 + there * 2, 0, 2),
            (low * 8 + lax.rem(there + 3, 4) * 2, 2, 1),
            (low * 8 + lax.rem(there + 1, 4) * 2 + 1, 3, 1),
        ):
            source = a_ref.at[:, pl.ds(pl.multiple_of(units * UNIT, UNIT), length * UNIT)]
            yield source, block.at[:, slot * UNIT : (slot + length) * UNIT]

    def a_start(dx, turn):
        low = z_lows[turn]
        for source, target in a_pieces(dx, low):
            if dx == 0 and turn == 0:
                pltpu.make_async_copy(source, target, a_recv.at[0, 0]).start()
            else:
                pltpu.make_async_remote_copy(
                    source, target, a_send.at[turn, dx // 2], a_recv.at[turn, dx // 2],
                    device_id=device(x + dx, y, z_high * 4 + low, core), device_id_type=MESH,
                ).start()

    def a_copy(dx, turn):
        block = a_all.at[z_lows[turn], pl.ds(ROWS * (dx // 2), ROWS)]
        if dx == 0 and turn == 0:
            return pltpu.make_async_copy(block, block, a_recv.at[0, 0])
        return pltpu.make_async_remote_copy(
            block, block, a_send.at[turn, dx // 2], a_recv.at[turn, dx // 2], device_id=mate, device_id_type=MESH
        )

    def b_place(half, i):
        high = 1 - z_high if half == 0 else z_high
        return high, lax.rem(y + OFFSETS[i], 4)

    def b_across(half, i):
        high, ys = b_place(half, i)
        return pltpu.make_async_remote_copy(
            b_ref.at[ys, high], b_all.at[high, ys, :, unit(2 + core)], bx_send.at[half, i], bx_recv.at[half, i],
            device_id=device(x + toward, y, z, core), device_id_type=MESH,
        )

    def b_forward(half, i, slot):
        high, ys = b_place(half, i)
        here = b_all.at[high, ys, :, unit(slot)]
        return pltpu.make_async_remote_copy(
            here, here, fw_send.at[half, i], fw_recv.at[half, i], device_id=mate, device_id_type=MESH
        )

    def b_own(half):
        high = 1 - z_high if half == 0 else z_high
        return pltpu.make_async_copy(b_ref.at[:, high], b_all.at[high, :, :, unit(core)], b_local.at[half])

    def b_mate(half, slot):
        high = 1 - z_high if half == 0 else z_high
        return pltpu.make_async_remote_copy(
            b_ref.at[:, high], b_all.at[high, :, :, unit(slot)], mate_send.at[half], mate_recv.at[half],
            device_id=mate, device_id_type=MESH,
        )

    a_start(0, 0)
    b_own(0).start()
    b_own(1).start()
    pl.semaphore_wait(barrier, len(partners))
    for i in range(4):
        b_across(0, i).start()
    b_mate(0, core).start()
    a_start(2, 0)
    for turn in (1, 2):
        for dx in (0, 2):
            a_start(dx, turn)
    for i in range(4):
        b_across(1, i).start()
    b_mate(1, core).start()
    for dx in (0, 2):
        a_start(dx, 3)

    steps = (4, 3 * sign, -3 * sign, 2 * sign, -2 * sign, sign, -sign, 0)
    turns = (0, 1, 2, 3, 3, 2, 1, 0)

    def multiply(b, i):
        to = lax.rem(z + steps[b] + 8, 8)
        ys = lax.rem(y + OFFSETS[i], 4)
        product = lax.dot_general(
            a_all[lax.rem(to, 4)], b_all[lax.div(to, 4), ys], (((1,), (1,)), ((), ())), preferred_element_type=jnp.float32
        )
        part[b, TOP[i]] = product[:ROWS]
        part[b, BOTTOM[i]] = product[ROWS:]

    def near_copy(b, d):
        return pltpu.make_async_remote_copy(
            part.at[b, pl.ds(2 * d, 2)], near.at[b, d], near_send.at[b, d], near_recv.at[b, d],
            device_id=device(x, y + 1 - 2 * d, z, core), device_id_type=MESH,
        )

    def far_copy(b, d):
        return pltpu.make_async_remote_copy(
            part.at[b, 4 + d], far.at[b, d], far_send.at[b, d], far_recv.at[b, d],
            device_id=device(x, y + 1 - 2 * d, z, core), device_id_type=MESH,
        )

    def z_first_copy(d):
        return pltpu.make_async_remote_copy(
            part.at[0, 6 + d], z_first.at[d], zf_send.at[d], zf_recv.at[d],
            device_id=device(x, y, z + 1 - 2 * d, core), device_id_type=MESH,
        )

    def z_ring_copy(b, d, step):
        return pltpu.make_async_remote_copy(
            part.at[b, pl.ds(6, 2)], z_ring.at[step, d], zr_send.at[step, d], zr_recv.at[step, d],
            device_id=device(x, y, z + 1 - 2 * d, core), device_id_type=MESH,
        )

    def z_last_copy(b, d, half):
        return pltpu.make_async_remote_copy(
            part.at[b, 6 + half], z_last.at[half, d], zl_send.at[half, d], zl_recv.at[half, d],
            device_id=device(x + 2 * half, y, z + 1 - 2 * d, core), device_id_type=MESH,
        )

    x_last_copy = pltpu.make_async_remote_copy(
        part.at[7, 7], x_last, xl_send, xl_recv, device_id=device(x + 2, y, z, core), device_id_type=MESH
    )

    def begin(b):
        turn = turns[b]
        if b < 4:
            for dx in (0, 2):
                if dx == 0 and turn == 0:
                    a_copy(0, 0).wait()
                else:
                    a_copy(dx, turn).wait_recv()
        half = {0: 0, 2: 1}.get(b)
        if half is not None:
            b_own(half).wait()
            b_mate(half, 1 - core).wait_recv()
        for i in range(4):
            if half is not None:
                b_across(half, i).wait_recv()
                b_forward(half, i, 2 + core).start()
                b_forward(half, i, 3 - core).wait_recv()
            multiply(b, i)
            if i in (1, 2):
                near_copy(b, i - 1).start()

    def pass_on(b):
        for d in range(2):
            near_copy(b, d).wait_recv()
            part[b, 4 + d] += near[b, d, 0]
            far_copy(b, d).start()

    def finish(b):
        for d in range(2):
            far_copy(b, d).wait_recv()
        part[b, 6] += far[b, 0] + near[b, 1, 1]
        part[b, 7] += far[b, 1] + near[b, 0, 1]
        d = way if b % 2 else 1 - way
        if b == 0:
            z_first_copy(0).start()
            z_first_copy(1).start()
        elif b < 3:
            z_first_copy(d).wait_recv()
            part[b, 6 + d] += z_first[d]
            z_ring_copy(b, d, 0).start()
        elif b < 7:
            step = (b - 3) // 2
            z_ring_copy(b, d, step).wait_recv()
            part[b, pl.ds(6, 2)] += z_ring[step, d]
            if step == 0:
                z_ring_copy(b, d, 1).start()
            else:
                z_last_copy(b, d, 1).start()
                z_last_copy(b, d, 0).start()
        else:
            x_last_copy.start()

    for t in range(BLOCKS + 2):
        if t < BLOCKS:
            begin(t)
        if 0 <= t - 1 < BLOCKS:
            pass_on(t - 1)
        if 0 <= t - 2:
            finish(t - 2)

    for half in range(2):
        for d in range(2):
            z_last_copy(5, d, half).wait_recv()
    x_last_copy.wait_recv()
    out_ref[...] = part[7, 6] + x_last[...] + z_last[0, 0] + z_last[0, 1] + z_last[1, 0] + z_last[1, 1]

    for turn in range(4):
        for dx in (0, 2):
            if turn or dx:
                a_copy(dx, turn).wait_send()
    for half in range(2):
        b_mate(half, core).wait_send()
        for i in range(4):
            b_across(half, i).wait_send()
            b_forward(half, i, 2 + core).wait_send()
    for b in range(BLOCKS):
        for d in range(2):
            near_copy(b, d).wait_send()
            far_copy(b, d).wait_send()
    for d in range(2):
        z_first_copy(d).wait_send()
        for step in range(2):
            z_ring_copy(1, d, step).wait_send()
        for half in range(2):
            z_last_copy(5, d, half).wait_send()
    x_last_copy.wait_send()


def local(amplitudes, integrals, residual_in):
    pieces = integrals.reshape(4, 2, COLS, UNIT)
    dma = pltpu.SemaphoreType.DMA
    ladder = pl.pallas_call(
        kernel,
        out_shape=jax.ShapeDtypeStruct((ROWS, COLS), jnp.float32),
        in_specs=[pl.BlockSpec(memory_space=pl.ANY)] * 2,
        out_specs=pl.BlockSpec(memory_space=pltpu.VMEM),
        scratch_shapes=[
            pltpu.VMEM((4, 2 * ROWS, DEPTH), jnp.bfloat16),
            pltpu.VMEM((2, 4, COLS, DEPTH), jnp.bfloat16),
            pltpu.VMEM((BLOCKS, 8, ROWS, COLS), jnp.float32),
            pltpu.VMEM((BLOCKS, 2, 2, ROWS, COLS), jnp.float32),
            pltpu.VMEM((BLOCKS, 2, ROWS, COLS), jnp.float32),
            pltpu.VMEM((2, ROWS, COLS), jnp.float32),
            pltpu.VMEM((2, 2, 2, ROWS, COLS), jnp.float32),
            pltpu.VMEM((2, 2, ROWS, COLS), jnp.float32),
            pltpu.VMEM((ROWS, COLS), jnp.float32),
            dma((4, 2)), dma((4, 2)), dma((2,)), dma((2,)), dma((2,)), dma((2, 4)), dma((2, 4)), dma((2, 4)), dma((2, 4)),
            dma((BLOCKS, 2)), dma((BLOCKS, 2)), dma((BLOCKS, 2)), dma((BLOCKS, 2)),
            dma((2,)), dma((2,)), dma((2, 2)), dma((2, 2)), dma((2, 2)), dma((2, 2)), dma(()), dma(()),
        ],
        compiler_params=pltpu.CompilerParams(collective_id=0, has_side_effects=True, vmem_limit_bytes=40 << 20),
        name="ladder",
    )(amplitudes, pieces)
    return residual_in + ladder


def solution(mesh):
    return jax.shard_map(
        local,
        mesh=mesh,
        in_specs=(P("row", "col"), P(None, ("col", "row")), P("row", "col")),
        out_specs=P("row", "col"),
        check_vma=False,
    )
```

```python
import functools

import jax
import jax.numpy as jnp
from jax import lax
from jax.experimental import pallas as pl
from jax.experimental.pallas import tpu as pltpu
from jax.sharding import PartitionSpec as P

MESH = pl.DeviceIdType.MESH
ROWS = 48
COLS = 256
UNIT = 256
DEPTH = 4 * UNIT
BLOCKS = 8
EARLY = 1
OFFSETS = (2, 1, 3, 0)
TOP = (0, 4, 3, 6)
BOTTOM = (2, 1, 5, 7)

OUTER = (4, 3, 0, -1, -3, 2, -2, 1)
INNER = (4, 3, 0, -1, -3, -2, 2, 1)
OUTER_TURNS = (2, 4, 4, 10, 6, 8, 8, 9)
INNER_TURNS = (2, 4, 4, 10, 6, 7, 8, 10)
SCHEDULE = {
    "init": [("b", 0, 0), ("b", 0, 1), ("m", 0), ("a", 2, 0), ("a", 0, 1), ("b", 0, 2), ("b", 0, 3), ("a", 2, 1),
             ("b", 1, 0), ("b", 1, 1), ("b", 1, 2), ("b", 1, 3), ("a", 0, 2), ("a", 0, 3), ("a", 2, 2), ("a", 2, 3)],
    ("end", 0): [("m", 1)],
}


def device(x, y, z, core):
    x, y, z = lax.rem(x + 4, 4), lax.rem(y + 4, 4), lax.rem(z + 8, 8)
    return (lax.rem(z, 4) * 8 + x * 2 + core, y * 2 + lax.div(z, 4))


def kernel(
    a_ref, b_ref, out_ref,
    a_all, b_all, part, near, far, z_first, z_ring, z_last, x_last,
    a_send, a_recv, b_local, mate_send, mate_recv, bx_send, bx_recv, fw_send, fw_recv,
    near_send, near_recv, far_send, far_recv, zf_send, zf_recv, zr_send, zr_recv, zl_send, zl_recv, xl_send, xl_recv,
):
    row, col = lax.axis_index("row"), lax.axis_index("col")
    core = lax.rem(row, 2)
    x = lax.rem(lax.div(row, 2), 4)
    z_low = lax.div(row, 8)
    y = lax.div(col, 2)
    z_high = lax.rem(col, 2)
    z = z_high * 4 + z_low
    mate = device(x, y, z, 1 - core)
    toward = 1 - 2 * core
    way = 1 - lax.rem(z_low, 2)
    sign = 1 - 2 * way
    outer = 1 - lax.rem(lax.div(z_low + 1, 2), 2)

    z_lows = (z_low, z_low + 1 - 2 * lax.rem(z_low, 2), 3 - z_low, lax.rem(z_low + 2, 4))

    barrier = pltpu.get_barrier_semaphore()
    partners = [mate, device(x + 1, y, z, core), device(x - 1, y, z, core)]
    partners += [device(x, y + 1, z, core), device(x, y - 1, z, core)]
    partners += [device(x + dx, y, z + dz, core) for dx in (0, 2) for dz in (1, -1)]
    partners += [device(x + dx, y, z_high * 4 + low, core) for low in z_lows for dx in (0, 2)][1:]
    for partner in partners:
        pl.semaphore_signal(barrier, inc=1, device_id=partner, device_id_type=MESH)

    def unit(start):
        return pl.ds(pl.multiple_of(start * UNIT, UNIT), UNIT)

    def a_pieces(dx, low):
        there = lax.rem(x + dx, 4)
        block = a_all.at[z_low, pl.ds(ROWS * (dx // 2), ROWS)]
        for units, slot, length in (
            (low * 8 + there * 2, 0, 2),
            (low * 8 + lax.rem(there + 3, 4) * 2, 2, 1),
            (low * 8 + lax.rem(there + 1, 4) * 2 + 1, 3, 1),
        ):
            source = a_ref.at[:, pl.ds(pl.multiple_of(units * UNIT, UNIT), length * UNIT)]
            yield source, block.at[:, slot * UNIT : (slot + length) * UNIT]

    def a_start(dx, turn):
        low = z_lows[turn]
        for source, target in a_pieces(dx, low):
            if dx == 0 and turn == 0:
                pltpu.make_async_copy(source, target, a_recv.at[0, 0]).start()
            else:
                pltpu.make_async_remote_copy(
                    source, target, a_send.at[turn, dx // 2], a_recv.at[turn, dx // 2],
                    device_id=device(x + dx, y, z_high * 4 + low, core), device_id_type=MESH,
                ).start()

    def a_copy(dx, turn):
        block = a_all.at[z_lows[turn], pl.ds(ROWS * (dx // 2), ROWS)]
        if dx == 0 and turn == 0:
            return pltpu.make_async_copy(block, block, a_recv.at[0, 0])
        return pltpu.make_async_remote_copy(
            block, block, a_send.at[turn, dx // 2], a_recv.at[turn, dx // 2], device_id=mate, device_id_type=MESH
        )

    def b_place(half, i):
        high = 1 - z_high if half == 0 else z_high
        return high, lax.rem(y + OFFSETS[i], 4)

    def b_across(half, i):
        high, ys = b_place(half, i)
        return pltpu.make_async_remote_copy(
            b_ref.at[ys, high], b_all.at[high, ys, :, unit(2 + core)], bx_send.at[half, i], bx_recv.at[half, i],
            device_id=device(x + toward, y, z, core), device_id_type=MESH,
        )

    def b_forward(half, i, slot):
        high, ys = b_place(half, i)
        here = b_all.at[high, ys, :, unit(slot)]
        return pltpu.make_async_remote_copy(
            here, here, fw_send.at[half, i], fw_recv.at[half, i], device_id=mate, device_id_type=MESH
        )

    def b_own(half):
        high = 1 - z_high if half == 0 else z_high
        return pltpu.make_async_copy(b_ref.at[:, high], b_all.at[high, :, :, unit(core)], b_local.at[half])

    def b_mate(half, slot):
        high = 1 - z_high if half == 0 else z_high
        return pltpu.make_async_remote_copy(
            b_ref.at[:, high], b_all.at[high, :, :, unit(slot)], mate_send.at[half], mate_recv.at[half],
            device_id=mate, device_id_type=MESH,
        )

    def run(when):
        for op in SCHEDULE.get(when, ()):
            if op[0] == "b":
                b_across(op[1], op[2]).start()
            elif op[0] == "m":
                b_mate(op[1], core).start()
            else:
                a_start(op[1], op[2])

    a_start(0, 0)
    b_own(0).start()
    b_own(1).start()
    pl.semaphore_wait(barrier, len(partners))
    run("init")

    steps = [sign * (step_out * outer + step_in * (1 - outer)) for step_out, step_in in zip(OUTER, INNER, strict=True)]

    def multiply(b, i):
        to = lax.rem(z + steps[b] + 8, 8)
        ys = lax.rem(y + OFFSETS[i], 4)
        product = lax.dot_general(
            a_all[lax.rem(to, 4)], b_all[lax.div(to, 4), ys], (((1,), (1,)), ((), ())), preferred_element_type=jnp.float32
        )
        part[b, TOP[i]] = product[:ROWS]
        part[b, BOTTOM[i]] = product[ROWS:]

    def near_copy(b, d):
        return pltpu.make_async_remote_copy(
            part.at[b, pl.ds(2 * d, 2)], near.at[b, d], near_send.at[b, d], near_recv.at[b, d],
            device_id=device(x, y + 1 - 2 * d, z, core), device_id_type=MESH,
        )

    def far_copy(b, d):
        return pltpu.make_async_remote_copy(
            part.at[b, 4 + d], far.at[b, d], far_send.at[b, d], far_recv.at[b, d],
            device_id=device(x, y + 1 - 2 * d, z, core), device_id_type=MESH,
        )

    def z_first_copy(d):
        return pltpu.make_async_remote_copy(
            part.at[0, 6 + d], z_first.at[d], zf_send.at[d], zf_recv.at[d],
            device_id=device(x, y, z + 1 - 2 * d, core), device_id_type=MESH,
        )

    def z_ring_copy(b, d, step):
        return pltpu.make_async_remote_copy(
            part.at[b, pl.ds(6, 2)], z_ring.at[step, d], zr_send.at[step, d], zr_recv.at[step, d],
            device_id=device(x, y, z + 1 - 2 * d, core), device_id_type=MESH,
        )

    def z_last_copy(b, d, half):
        return pltpu.make_async_remote_copy(
            part.at[b, 6 + half], z_last.at[half, d], zl_send.at[half, d], zl_recv.at[half, d],
            device_id=device(x + 2 * half, y, z + 1 - 2 * d, core), device_id_type=MESH,
        )

    x_last_copy = pltpu.make_async_remote_copy(
        part.at[2, 7], x_last, xl_send, xl_recv, device_id=device(x + 2, y, z, core), device_id_type=MESH
    )

    def forward(half, i):
        b_across(half, i).wait_recv()
        b_forward(half, i, 2 + core).start()
        run(("got", half, i))

    def begin(b):
        turn = {0: 0, 1: 1, 4: 2, 5: 3}.get(b)
        if turn == 0:
            a_copy(0, 0).wait()
            a_copy(2, 0).wait_recv()
        elif turn is not None:
            a_copy(0, turn).wait_recv()
            a_copy(2, turn).wait_recv()

        half = {0: 0, 2: 1}.get(b)
        if half is not None:
            b_own(half).wait()
            b_mate(half, 1 - core).wait_recv()
        for i in range(4):
            if half is not None:
                if b == 0 or i >= EARLY:
                    forward(half, i)
                b_forward(half, i, 3 - core).wait_recv()
            multiply(b, i)
            if i in (1, 2):
                near_copy(b, i - 1).start()
        run(("end", b))

    def pass_on(b):
        for d in range(2):
            near_copy(b, d).wait_recv()
            part[b, 4 + d] += near[b, d, 0]
            far_copy(b, d).start()

    def finish(b):
        for d in range(2):
            far_copy(b, d).wait_recv()
        part[b, 6] += far[b, 0] + near[b, 1, 1]
        part[b, 7] += far[b, 1] + near[b, 0, 1]
    def along_z(b, step):
        d = way if step > 0 else 1 - way
        if step == 4:
            z_first_copy(0).start()
            z_first_copy(1).start()
        elif abs(step) == 3:
            z_first_copy(d).wait_recv()
            part[b, 6 + d] += z_first[d]
            z_ring_copy(b, d, 0).start()
        elif step:
            z_ring_copy(b, d, 2 - abs(step)).wait_recv()
            part[b, pl.ds(6, 2)] += z_ring[2 - abs(step), d]
            if abs(step) == 2:
                z_ring_copy(b, d, 1).start()
            else:
                z_last_copy(b, d, 1).start()
                z_last_copy(b, d, 0).start()
        else:
            x_last_copy.start()

    def move(t, steps, turns):
        for b in sorted(range(BLOCKS), key=lambda b: (-abs(steps[b]), b)):
            if turns[b] == t:
                along_z(b, steps[b])

    for t in range(max(OUTER_TURNS + INNER_TURNS) + 1):
        if t < BLOCKS:
            begin(t)
        if 0 <= t - 1 < BLOCKS:
            pass_on(t - 1)
        if t == 1:
            for i in range(EARLY):
                forward(1, i)
        if 0 <= t - 2 < BLOCKS:
            finish(t - 2)
        pl.when(outer == 1)(functools.partial(move, t, OUTER, OUTER_TURNS))
        pl.when(outer == 0)(functools.partial(move, t, INNER, INNER_TURNS))

    for half in range(2):
        for d in range(2):
            z_last_copy(5, d, half).wait_recv()
    x_last_copy.wait_recv()
    out_ref[...] = part[2, 6] + x_last[...] + z_last[0, 0] + z_last[0, 1] + z_last[1, 0] + z_last[1, 1]

    for turn in range(4):
        for dx in (0, 2):
            if turn or dx:
                a_copy(dx, turn).wait_send()
    for half in range(2):
        b_mate(half, core).wait_send()
        for i in range(4):
            b_across(half, i).wait_send()
            b_forward(half, i, 2 + core).wait_send()
    for b in range(BLOCKS):
        for d in range(2):
            near_copy(b, d).wait_send()
            far_copy(b, d).wait_send()
    for d in range(2):
        z_first_copy(d).wait_send()
        for step in range(2):
            z_ring_copy(1, d, step).wait_send()
        for half in range(2):
            z_last_copy(5, d, half).wait_send()
    x_last_copy.wait_send()


def local(amplitudes, integrals, residual_in):
    pieces = integrals.reshape(4, 2, COLS, UNIT)
    dma = pltpu.SemaphoreType.DMA
    ladder = pl.pallas_call(
        kernel,
        out_shape=jax.ShapeDtypeStruct((ROWS, COLS), jnp.float32),
        in_specs=[pl.BlockSpec(memory_space=pl.ANY)] * 2,
        out_specs=pl.BlockSpec(memory_space=pltpu.VMEM),
        scratch_shapes=[
            pltpu.VMEM((4, 2 * ROWS, DEPTH), jnp.bfloat16),
            pltpu.VMEM((2, 4, COLS, DEPTH), jnp.bfloat16),
            pltpu.VMEM((BLOCKS, 8, ROWS, COLS), jnp.float32),
            pltpu.VMEM((BLOCKS, 2, 2, ROWS, COLS), jnp.float32),
            pltpu.VMEM((BLOCKS, 2, ROWS, COLS), jnp.float32),
            pltpu.VMEM((2, ROWS, COLS), jnp.float32),
            pltpu.VMEM((2, 2, 2, ROWS, COLS), jnp.float32),
            pltpu.VMEM((2, 2, ROWS, COLS), jnp.float32),
            pltpu.VMEM((ROWS, COLS), jnp.float32),
            dma((4, 2)), dma((4, 2)), dma((2,)), dma((2,)), dma((2,)), dma((2, 4)), dma((2, 4)), dma((2, 4)), dma((2, 4)),
            dma((BLOCKS, 2)), dma((BLOCKS, 2)), dma((BLOCKS, 2)), dma((BLOCKS, 2)),
            dma((2,)), dma((2,)), dma((2, 2)), dma((2, 2)), dma((2, 2)), dma((2, 2)), dma(()), dma(()),
        ],
        compiler_params=pltpu.CompilerParams(collective_id=0, has_side_effects=True, vmem_limit_bytes=60 << 20),
        name="ladder",
    )(amplitudes, pieces)
    return residual_in + ladder


def solution(mesh):
    return jax.shard_map(
        local,
        mesh=mesh,
        in_specs=(P("row", "col"), P(None, ("col", "row")), P("row", "col")),
        out_specs=P("row", "col"),
        check_vma=False,
    )
```

```python
import functools

import jax
import jax.numpy as jnp
from jax import lax
from jax.experimental import pallas as pl
from jax.experimental.pallas import tpu as pltpu
from jax.sharding import PartitionSpec as P

MESH = pl.DeviceIdType.MESH
ROWS = 48
COLS = 256
UNIT = 256
DEPTH = 4 * UNIT
BLOCKS = 8
OFFSETS = (2, 1, 3, 0)
TOP = (0, 4, 3, 6)
BOTTOM = (2, 1, 5, 7)

OUTER = (4, 3, 0, -1, -3, 2, -2, 1)
INNER = (4, 3, 0, -1, -3, -2, 2, 1)
OUTER_TURNS = (2, 4, 4, 10, 6, 8, 8, 9)
INNER_TURNS = (2, 4, 4, 10, 6, 7, 8, 10)
SCHEDULE = {
    "init": [("b", 0, 0), ("m", 0), ("a", 2, 0), ("a", 0, 1), ("b", 0, 1), ("a", 2, 1), ("b", 0, 2), ("b", 0, 3), ("a", 0, 2), ("a", 0, 3)],
    ("got", 0, 0): [("b", 1, 0), ("b", 1, 1), ("b", 1, 2), ("b", 1, 3)],
    ("got", 0, 3): [("m", 1), ("a", 2, 2)],
    ("got", 1, 0): [("a", 2, 3)],
}


def device(x, y, z, core):
    x, y, z = lax.rem(x + 4, 4), lax.rem(y + 4, 4), lax.rem(z + 8, 8)
    return (lax.rem(z, 4) * 8 + x * 2 + core, y * 2 + lax.div(z, 4))


def kernel(
    a_ref, b_ref, out_ref,
    a_all, b_all, part, near, far, z_first, z_ring, z_last, x_last,
    a_send, a_recv, b_local, mate_send, mate_recv, bx_send, bx_recv, fw_send, fw_recv,
    near_send, near_recv, far_send, far_recv, zf_send, zf_recv, zr_send, zr_recv, zl_send, zl_recv, xl_send, xl_recv,
):
    row, col = lax.axis_index("row"), lax.axis_index("col")
    core = lax.rem(row, 2)
    x = lax.rem(lax.div(row, 2), 4)
    z_low = lax.div(row, 8)
    y = lax.div(col, 2)
    z_high = lax.rem(col, 2)
    z = z_high * 4 + z_low
    mate = device(x, y, z, 1 - core)
    toward = 1 - 2 * core
    way = 1 - lax.rem(z_low, 2)
    sign = 1 - 2 * way
    outer = 1 - lax.rem(lax.div(z_low + 1, 2), 2)

    z_lows = (z_low, z_low + 1 - 2 * lax.rem(z_low, 2), 3 - z_low, lax.rem(z_low + 2, 4))

    barrier = pltpu.get_barrier_semaphore()
    partners = [mate, device(x + 1, y, z, core), device(x - 1, y, z, core)]
    partners += [device(x, y + 1, z, core), device(x, y - 1, z, core)]
    partners += [device(x + dx, y, z + dz, core) for dx in (0, 2) for dz in (1, -1)]
    partners += [device(x + dx, y, z_high * 4 + low, core) for low in z_lows for dx in (0, 2)][1:]
    for partner in partners:
        pl.semaphore_signal(barrier, inc=1, device_id=partner, device_id_type=MESH)

    def unit(start):
        return pl.ds(pl.multiple_of(start * UNIT, UNIT), UNIT)

    def a_pieces(dx, low):
        there = lax.rem(x + dx, 4)
        block = a_all.at[z_low, pl.ds(ROWS * (dx // 2), ROWS)]
        for units, slot, length in (
            (low * 8 + there * 2, 0, 2),
            (low * 8 + lax.rem(there + 3, 4) * 2, 2, 1),
            (low * 8 + lax.rem(there + 1, 4) * 2 + 1, 3, 1),
        ):
            source = a_ref.at[:, pl.ds(pl.multiple_of(units * UNIT, UNIT), length * UNIT)]
            yield source, block.at[:, slot * UNIT : (slot + length) * UNIT]

    def a_start(dx, turn):
        low = z_lows[turn]
        for source, target in a_pieces(dx, low):
            if dx == 0 and turn == 0:
                pltpu.make_async_copy(source, target, a_recv.at[0, 0]).start()
            else:
                pltpu.make_async_remote_copy(
                    source, target, a_send.at[turn, dx // 2], a_recv.at[turn, dx // 2],
                    device_id=device(x + dx, y, z_high * 4 + low, core), device_id_type=MESH,
                ).start()

    def a_copy(dx, turn):
        block = a_all.at[z_lows[turn], pl.ds(ROWS * (dx // 2), ROWS)]
        if dx == 0 and turn == 0:
            return pltpu.make_async_copy(block, block, a_recv.at[0, 0])
        return pltpu.make_async_remote_copy(
            block, block, a_send.at[turn, dx // 2], a_recv.at[turn, dx // 2], device_id=mate, device_id_type=MESH
        )

    def b_place(half, i):
        high = 1 - z_high if half == 0 else z_high
        return high, lax.rem(y + OFFSETS[i], 4)

    def b_across(half, i):
        high, ys = b_place(half, i)
        return pltpu.make_async_remote_copy(
            b_ref.at[ys, high], b_all.at[high, ys, :, unit(2 + core)], bx_send.at[half, i], bx_recv.at[half, i],
            device_id=device(x + toward, y, z, core), device_id_type=MESH,
        )

    def b_forward(half, i, slot):
        high, ys = b_place(half, i)
        here = b_all.at[high, ys, :, unit(slot)]
        return pltpu.make_async_remote_copy(
            here, here, fw_send.at[half, i], fw_recv.at[half, i], device_id=mate, device_id_type=MESH
        )

    def b_own(half):
        high = 1 - z_high if half == 0 else z_high
        return pltpu.make_async_copy(b_ref.at[:, high], b_all.at[high, :, :, unit(core)], b_local.at[half])

    def b_mate(half, slot):
        high = 1 - z_high if half == 0 else z_high
        return pltpu.make_async_remote_copy(
            b_ref.at[:, high], b_all.at[high, :, :, unit(slot)], mate_send.at[half], mate_recv.at[half],
            device_id=mate, device_id_type=MESH,
        )

    def run(when):
        for op in SCHEDULE.get(when, ()):
            if op[0] == "b":
                b_across(op[1], op[2]).start()
            elif op[0] == "m":
                b_mate(op[1], core).start()
            else:
                a_start(op[1], op[2])

    a_start(0, 0)
    b_own(0).start()
    b_own(1).start()
    pl.semaphore_wait(barrier, len(partners))
    run("init")

    steps = [sign * (step_out * outer + step_in * (1 - outer)) for step_out, step_in in zip(OUTER, INNER, strict=True)]

    def multiply(b, i):
        to = lax.rem(z + steps[b] + 8, 8)
        ys = lax.rem(y + OFFSETS[i], 4)
        product = lax.dot_general(
            a_all[lax.rem(to, 4)], b_all[lax.div(to, 4), ys], (((1,), (1,)), ((), ())), preferred_element_type=jnp.float32
        )
        part[b, TOP[i]] = product[:ROWS]
        part[b, BOTTOM[i]] = product[ROWS:]

    def near_copy(b, d, place):
        return pltpu.make_async_remote_copy(
            part.at[b, 2 * d + place], near.at[b, d, place], near_send.at[b, d, place], near_recv.at[b, d, place],
            device_id=device(x, y + 1 - 2 * d, z, core), device_id_type=MESH,
        )

    def far_copy(b, d):
        return pltpu.make_async_remote_copy(
            part.at[b, 4 + d], far.at[b, d], far_send.at[b, d], far_recv.at[b, d],
            device_id=device(x, y + 1 - 2 * d, z, core), device_id_type=MESH,
        )

    def z_first_copy(d):
        return pltpu.make_async_remote_copy(
            part.at[0, 6 + d], z_first.at[d], zf_send.at[d], zf_recv.at[d],
            device_id=device(x, y, z + 1 - 2 * d, core), device_id_type=MESH,
        )

    def z_ring_copy(b, d, step):
        return pltpu.make_async_remote_copy(
            part.at[b, pl.ds(6, 2)], z_ring.at[step, d], zr_send.at[step, d], zr_recv.at[step, d],
            device_id=device(x, y, z + 1 - 2 * d, core), device_id_type=MESH,
        )

    def z_last_copy(b, d, half):
        return pltpu.make_async_remote_copy(
            part.at[b, 6 + half], z_last.at[half, d], zl_send.at[half, d], zl_recv.at[half, d],
            device_id=device(x + 2 * half, y, z + 1 - 2 * d, core), device_id_type=MESH,
        )

    x_last_copy = pltpu.make_async_remote_copy(
        part.at[2, 7], x_last, xl_send, xl_recv, device_id=device(x + 2, y, z, core), device_id_type=MESH
    )

    def forward(half, i):
        b_across(half, i).wait_recv()
        b_forward(half, i, 2 + core).start()
        run(("got", half, i))

    def chunk(b, i):
        multiply(b, i)
        if i == 0:
            near_copy(b, 0, 0).start()
            near_copy(b, 1, 0).start()
        elif i < 3:
            near_copy(b, i - 1, 1).start()

    def got_a(turn):
        if turn:
            a_copy(0, turn).wait_recv()
        else:
            a_copy(0, 0).wait()
        a_copy(2, turn).wait_recv()

    def got_b(half, i):
        if i == 0:
            b_own(half).wait()
            b_mate(half, 1 - core).wait_recv()
        forward(half, i)
        b_forward(half, i, 3 - core).wait_recv()

    def begin(b):
        for i in range(4):
            chunk(b, i)

    def pass_on(b):
        for d in range(2):
            near_copy(b, d, 0).wait_recv()
            part[b, 4 + d] += near[b, d, 0]
            far_copy(b, d).start()

    def finish(b):
        for d in range(2):
            far_copy(b, d).wait_recv()
            near_copy(b, d, 1).wait_recv()
        part[b, 6] += far[b, 0] + near[b, 1, 1]
        part[b, 7] += far[b, 1] + near[b, 0, 1]
    def along_z(b, step):
        d = way if step > 0 else 1 - way
        if step == 4:
            z_first_copy(0).start()
            z_first_copy(1).start()
        elif abs(step) == 3:
            z_first_copy(d).wait_recv()
            part[b, 6 + d] += z_first[d]
            z_ring_copy(b, d, 0).start()
        elif step:
            z_ring_copy(b, d, 2 - abs(step)).wait_recv()
            part[b, pl.ds(6, 2)] += z_ring[2 - abs(step), d]
            if abs(step) == 2:
                z_ring_copy(b, d, 1).start()
            else:
                z_last_copy(b, d, 1).start()
                z_last_copy(b, d, 0).start()
        else:
            x_last_copy.start()

    def move(t, steps, turns):
        for b in sorted(range(BLOCKS), key=lambda b: (-abs(steps[b]), b)):
            if turns[b] == t:
                along_z(b, steps[b])

    def settle(b):
        if b < BLOCKS:
            finish(b)
        pl.when(outer == 1)(functools.partial(move, b + 2, OUTER, OUTER_TURNS))
        pl.when(outer == 0)(functools.partial(move, b + 2, INNER, INNER_TURNS))

    got_a(0)
    got_b(0, 0)
    chunk(0, 0)
    got_b(0, 1)
    chunk(0, 1)
    got_a(1)
    chunk(1, 0)
    chunk(1, 1)
    got_b(0, 2)
    chunk(0, 2)
    chunk(1, 2)
    pass_on(0)
    got_b(0, 3)
    chunk(0, 3)
    chunk(1, 3)
    pass_on(1)
    for i in range(4):
        got_b(1, i)
        chunk(2, i)
        chunk(3, i)
        if i == 1:
            settle(0)
        if i == 2:
            settle(1)
            pass_on(2)
    pass_on(3)
    got_a(2)
    begin(4)
    settle(2)
    got_a(3)
    begin(5)
    pass_on(4)
    settle(3)
    begin(6)
    pass_on(5)
    settle(4)
    begin(7)
    pass_on(6)
    settle(5)
    pass_on(7)
    settle(6)
    settle(7)
    settle(8)

    for half in range(2):
        for d in range(2):
            z_last_copy(5, d, half).wait_recv()
    x_last_copy.wait_recv()
    out_ref[...] = part[2, 6] + x_last[...] + z_last[0, 0] + z_last[0, 1] + z_last[1, 0] + z_last[1, 1]

    for turn in range(4):
        for dx in (0, 2):
            if turn or dx:
                a_copy(dx, turn).wait_send()
    for half in range(2):
        b_mate(half, core).wait_send()
        for i in range(4):
            b_across(half, i).wait_send()
            b_forward(half, i, 2 + core).wait_send()
    for b in range(BLOCKS):
        for d in range(2):
            near_copy(b, d, 0).wait_send()
            near_copy(b, d, 1).wait_send()
            far_copy(b, d).wait_send()
    for d in range(2):
        z_first_copy(d).wait_send()
        for step in range(2):
            z_ring_copy(1, d, step).wait_send()
        for half in range(2):
            z_last_copy(5, d, half).wait_send()
    x_last_copy.wait_send()


def local(amplitudes, integrals, residual_in):
    pieces = integrals.reshape(4, 2, COLS, UNIT)
    dma = pltpu.SemaphoreType.DMA
    ladder = pl.pallas_call(
        kernel,
        out_shape=jax.ShapeDtypeStruct((ROWS, COLS), jnp.float32),
        in_specs=[pl.BlockSpec(memory_space=pl.ANY)] * 2,
        out_specs=pl.BlockSpec(memory_space=pltpu.VMEM),
        scratch_shapes=[
            pltpu.VMEM((4, 2 * ROWS, DEPTH), jnp.bfloat16),
            pltpu.VMEM((2, 4, COLS, DEPTH), jnp.bfloat16),
            pltpu.VMEM((BLOCKS, 8, ROWS, COLS), jnp.float32),
            pltpu.VMEM((BLOCKS, 2, 2, ROWS, COLS), jnp.float32),
            pltpu.VMEM((BLOCKS, 2, ROWS, COLS), jnp.float32),
            pltpu.VMEM((2, ROWS, COLS), jnp.float32),
            pltpu.VMEM((2, 2, 2, ROWS, COLS), jnp.float32),
            pltpu.VMEM((2, 2, ROWS, COLS), jnp.float32),
            pltpu.VMEM((ROWS, COLS), jnp.float32),
            dma((4, 2)), dma((4, 2)), dma((2,)), dma((2,)), dma((2,)), dma((2, 4)), dma((2, 4)), dma((2, 4)), dma((2, 4)),
            dma((BLOCKS, 2, 2)), dma((BLOCKS, 2, 2)), dma((BLOCKS, 2)), dma((BLOCKS, 2)),
            dma((2,)), dma((2,)), dma((2, 2)), dma((2, 2)), dma((2, 2)), dma((2, 2)), dma(()), dma(()),
        ],
        compiler_params=pltpu.CompilerParams(collective_id=0, has_side_effects=True, vmem_limit_bytes=60 << 20),
        name="ladder",
    )(amplitudes, pieces)
    return residual_in + ladder


def solution(mesh):
    return jax.shard_map(
        local,
        mesh=mesh,
        in_specs=(P("row", "col"), P(None, ("col", "row")), P("row", "col")),
        out_specs=P("row", "col"),
        check_vma=False,
    )
```

```python
import functools

import jax
import jax.numpy as jnp
from jax import lax
from jax.experimental import pallas as pl
from jax.experimental.pallas import tpu as pltpu
from jax.sharding import PartitionSpec as P

MESH = pl.DeviceIdType.MESH
ROWS = 48
COLS = 256
UNIT = 256
DEPTH = 4 * UNIT
BLOCKS = 8
OFFSETS = (2, 1, 3, 0)
TOP = (0, 4, 3, 6)
BOTTOM = (2, 1, 5, 7)

OUTER = (4, 3, 0, -1, -3, 2, -2, 1)
INNER = (4, 3, 0, -1, -3, -2, 2, 1)
OUTER_TURNS = (2, 4, 4, 10, 6, 8, 8, 9)
INNER_TURNS = (2, 4, 4, 10, 6, 7, 8, 10)
SCHEDULE = {
    "init": [("b", 0, 0), ("m", 0), ("a", 2, 0), ("a", 0, 1), ("b", 0, 1), ("a", 2, 1), ("b", 0, 2), ("b", 0, 3), ("b", 1, 0), ("a", 0, 2), ("a", 0, 3)],
    ("got", 0, 0): [("b", 1, 1), ("b", 1, 2), ("b", 1, 3)],
    ("got", 0, 3): [("m", 1), ("a", 2, 2)],
    ("got", 1, 0): [("a", 2, 3)],
}


def device(x, y, z, core):
    x, y, z = lax.rem(x + 4, 4), lax.rem(y + 4, 4), lax.rem(z + 8, 8)
    return (lax.rem(z, 4) * 8 + x * 2 + core, y * 2 + lax.div(z, 4))


def kernel(
    a_ref, b_ref, out_ref,
    a_all, b_all, part, near, far, z_first, z_ring, z_last, x_last,
    a_send, a_recv, b_local, mate_send, mate_recv, bx_send, bx_recv, fw_send, fw_recv,
    near_send, near_recv, far_send, far_recv, zf_send, zf_recv, zr_send, zr_recv, zl_send, zl_recv, xl_send, xl_recv,
):
    row, col = lax.axis_index("row"), lax.axis_index("col")
    core = lax.rem(row, 2)
    x = lax.rem(lax.div(row, 2), 4)
    z_low = lax.div(row, 8)
    y = lax.div(col, 2)
    z_high = lax.rem(col, 2)
    z = z_high * 4 + z_low
    mate = device(x, y, z, 1 - core)
    toward = 1 - 2 * core
    way = 1 - lax.rem(z_low, 2)
    sign = 1 - 2 * way
    outer = 1 - lax.rem(lax.div(z_low + 1, 2), 2)

    z_lows = (z_low, z_low + 1 - 2 * lax.rem(z_low, 2), 3 - z_low, lax.rem(z_low + 2, 4))

    barrier = pltpu.get_barrier_semaphore()
    partners = [mate, device(x + 1, y, z, core), device(x - 1, y, z, core)]
    partners += [device(x, y + 1, z, core), device(x, y - 1, z, core)]
    partners += [device(x + dx, y, z + dz, core) for dx in (0, 2) for dz in (1, -1)]
    partners += [device(x + dx, y, z_high * 4 + low, core) for low in z_lows for dx in (0, 2)][1:]
    for partner in partners:
        pl.semaphore_signal(barrier, inc=1, device_id=partner, device_id_type=MESH)

    def unit(start):
        return pl.ds(pl.multiple_of(start * UNIT, UNIT), UNIT)

    def a_pieces(dx, low):
        there = lax.rem(x + dx, 4)
        block = a_all.at[z_low, pl.ds(ROWS * (dx // 2), ROWS)]
        for units, slot, length in (
            (low * 8 + there * 2, 0, 2),
            (low * 8 + lax.rem(there + 3, 4) * 2, 2, 1),
            (low * 8 + lax.rem(there + 1, 4) * 2 + 1, 3, 1),
        ):
            source = a_ref.at[:, pl.ds(pl.multiple_of(units * UNIT, UNIT), length * UNIT)]
            yield source, block.at[:, slot * UNIT : (slot + length) * UNIT]

    def a_start(dx, turn):
        low = z_lows[turn]
        for source, target in a_pieces(dx, low):
            if dx == 0 and turn == 0:
                pltpu.make_async_copy(source, target, a_recv.at[0, 0]).start()
            else:
                pltpu.make_async_remote_copy(
                    source, target, a_send.at[turn, dx // 2], a_recv.at[turn, dx // 2],
                    device_id=device(x + dx, y, z_high * 4 + low, core), device_id_type=MESH,
                ).start()

    def a_copy(dx, turn):
        block = a_all.at[z_lows[turn], pl.ds(ROWS * (dx // 2), ROWS)]
        if dx == 0 and turn == 0:
            return pltpu.make_async_copy(block, block, a_recv.at[0, 0])
        return pltpu.make_async_remote_copy(
            block, block, a_send.at[turn, dx // 2], a_recv.at[turn, dx // 2], device_id=mate, device_id_type=MESH
        )

    def b_place(half, i):
        high = 1 - z_high if half == 0 else z_high
        return high, lax.rem(y + OFFSETS[i], 4)

    def b_across(half, i):
        high, ys = b_place(half, i)
        return pltpu.make_async_remote_copy(
            b_ref.at[ys, high], b_all.at[high, ys, :, unit(2 + core)], bx_send.at[half, i], bx_recv.at[half, i],
            device_id=device(x + toward, y, z, core), device_id_type=MESH,
        )

    def b_forward(half, i, slot):
        high, ys = b_place(half, i)
        here = b_all.at[high, ys, :, unit(slot)]
        return pltpu.make_async_remote_copy(
            here, here, fw_send.at[half, i], fw_recv.at[half, i], device_id=mate, device_id_type=MESH
        )

    def b_own(half):
        high = 1 - z_high if half == 0 else z_high
        return pltpu.make_async_copy(b_ref.at[:, high], b_all.at[high, :, :, unit(core)], b_local.at[half])

    def b_mate(half, slot):
        high = 1 - z_high if half == 0 else z_high
        return pltpu.make_async_remote_copy(
            b_ref.at[:, high], b_all.at[high, :, :, unit(slot)], mate_send.at[half], mate_recv.at[half],
            device_id=mate, device_id_type=MESH,
        )

    def run(when):
        for op in SCHEDULE.get(when, ()):
            if op[0] == "b":
                b_across(op[1], op[2]).start()
            elif op[0] == "m":
                b_mate(op[1], core).start()
            else:
                a_start(op[1], op[2])

    a_start(0, 0)
    b_own(0).start()
    b_own(1).start()
    pl.semaphore_wait(barrier, len(partners))
    run("init")

    steps = [sign * (step_out * outer + step_in * (1 - outer)) for step_out, step_in in zip(OUTER, INNER, strict=True)]

    def multiply(b, i):
        to = lax.rem(z + steps[b] + 8, 8)
        ys = lax.rem(y + OFFSETS[i], 4)
        product = lax.dot_general(
            a_all[lax.rem(to, 4)], b_all[lax.div(to, 4), ys], (((1,), (1,)), ((), ())), preferred_element_type=jnp.float32
        )
        part[b, TOP[i]] = product[:ROWS]
        part[b, BOTTOM[i]] = product[ROWS:]

    def near_copy(b, d, place):
        return pltpu.make_async_remote_copy(
            part.at[b, 2 * d + place], near.at[b, d, place], near_send.at[b, d, place], near_recv.at[b, d, place],
            device_id=device(x, y + 1 - 2 * d, z, core), device_id_type=MESH,
        )

    def far_copy(b, d):
        return pltpu.make_async_remote_copy(
            part.at[b, 4 + d], far.at[b, d], far_send.at[b, d], far_recv.at[b, d],
            device_id=device(x, y + 1 - 2 * d, z, core), device_id_type=MESH,
        )

    def z_first_copy(d):
        return pltpu.make_async_remote_copy(
            part.at[0, 6 + d], z_first.at[d], zf_send.at[d], zf_recv.at[d],
            device_id=device(x, y, z + 1 - 2 * d, core), device_id_type=MESH,
        )

    def z_ring_copy(b, d, step, half):
        return pltpu.make_async_remote_copy(
            part.at[b, 6 + half], z_ring.at[step, d, half], zr_send.at[step, d, half], zr_recv.at[step, d, half],
            device_id=device(x, y, z + 1 - 2 * d, core), device_id_type=MESH,
        )

    def z_last_copy(b, d, half):
        return pltpu.make_async_remote_copy(
            part.at[b, 6 + half], z_last.at[half, d], zl_send.at[half, d], zl_recv.at[half, d],
            device_id=device(x + 2 * half, y, z + 1 - 2 * d, core), device_id_type=MESH,
        )

    x_last_copy = pltpu.make_async_remote_copy(
        part.at[2, 7], x_last, xl_send, xl_recv, device_id=device(x + 2, y, z, core), device_id_type=MESH
    )

    def forward(half, i):
        b_across(half, i).wait_recv()
        b_forward(half, i, 2 + core).start()
        run(("got", half, i))

    def chunk(b, i):
        multiply(b, i)
        if i == 0:
            near_copy(b, 0, 0).start()
            near_copy(b, 1, 0).start()
        elif i < 3:
            near_copy(b, i - 1, 1).start()

    def got_a(turn):
        if turn:
            a_copy(0, turn).wait_recv()
        else:
            a_copy(0, 0).wait()
        a_copy(2, turn).wait_recv()

    def got_b(half, i):
        if i == 0:
            b_own(half).wait()
            b_mate(half, 1 - core).wait_recv()
        forward(half, i)
        b_forward(half, i, 3 - core).wait_recv()

    def begin(b):
        for i in range(4):
            chunk(b, i)

    def pass_on(b):
        for d in range(2):
            near_copy(b, d, 0).wait_recv()
            part[b, 4 + d] += near[b, d, 0]
            far_copy(b, d).start()

    def finish(b):
        for d in range(2):
            far_copy(b, d).wait_recv()
            near_copy(b, d, 1).wait_recv()
        part[b, 6] += far[b, 0] + near[b, 1, 1]
        part[b, 7] += far[b, 1] + near[b, 0, 1]
    def along_z(b, step):
        d = way if step > 0 else 1 - way
        if step == 4:
            z_first_copy(0).start()
            z_first_copy(1).start()
        elif abs(step) == 3:
            z_ring_copy(b, d, 0, 1 - d).start()
            z_first_copy(d).wait_recv()
            part[b, 6 + d] += z_first[d]
            z_ring_copy(b, d, 0, d).start()
        elif step:
            for half in (1, 0):
                z_ring_copy(b, d, 2 - abs(step), half).wait_recv()
                part[b, 6 + half] += z_ring[2 - abs(step), d, half]
                if abs(step) == 2:
                    z_ring_copy(b, d, 1, half).start()
                else:
                    z_last_copy(b, d, half).start()
        else:
            x_last_copy.start()

    def move(t, steps, turns):
        for b in sorted(range(BLOCKS), key=lambda b: (-abs(steps[b]), b)):
            if turns[b] == t:
                along_z(b, steps[b])

    def settle(b):
        if b < BLOCKS:
            finish(b)
        pl.when(outer == 1)(functools.partial(move, b + 2, OUTER, OUTER_TURNS))
        pl.when(outer == 0)(functools.partial(move, b + 2, INNER, INNER_TURNS))

    got_a(0)
    got_b(0, 0)
    chunk(0, 0)
    got_b(0, 1)
    chunk(0, 1)
    got_a(1)
    chunk(1, 0)
    chunk(1, 1)
    got_b(0, 2)
    chunk(0, 2)
    chunk(1, 2)
    pass_on(0)
    got_b(0, 3)
    chunk(0, 3)
    chunk(1, 3)
    pass_on(1)
    for i in range(4):
        got_b(1, i)
        chunk(2, i)
        chunk(3, i)
        if i == 1:
            settle(0)
        if i == 2:
            settle(1)
            pass_on(2)
    pass_on(3)
    got_a(2)
    begin(4)
    got_a(3)
    begin(5)
    settle(2)
    pass_on(4)
    begin(6)
    settle(3)
    pass_on(5)
    begin(7)
    settle(4)
    pass_on(6)
    settle(5)
    pass_on(7)
    settle(6)
    settle(7)
    settle(8)

    for half in range(2):
        for d in range(2):
            z_last_copy(5, d, half).wait_recv()
    x_last_copy.wait_recv()
    out_ref[...] = part[2, 6] + x_last[...] + z_last[0, 0] + z_last[0, 1] + z_last[1, 0] + z_last[1, 1]

    for turn in range(4):
        for dx in (0, 2):
            if turn or dx:
                a_copy(dx, turn).wait_send()
    for half in range(2):
        b_mate(half, core).wait_send()
        for i in range(4):
            b_across(half, i).wait_send()
            b_forward(half, i, 2 + core).wait_send()
    for b in range(BLOCKS):
        for d in range(2):
            near_copy(b, d, 0).wait_send()
            near_copy(b, d, 1).wait_send()
            far_copy(b, d).wait_send()
    for d in range(2):
        z_first_copy(d).wait_send()
        for step in range(2):
            for half in range(2):
                z_ring_copy(1, d, step, half).wait_send()
        for half in range(2):
            z_last_copy(5, d, half).wait_send()
    x_last_copy.wait_send()


def local(amplitudes, integrals, residual_in):
    pieces = integrals.reshape(4, 2, COLS, UNIT)
    dma = pltpu.SemaphoreType.DMA
    ladder = pl.pallas_call(
        kernel,
        out_shape=jax.ShapeDtypeStruct((ROWS, COLS), jnp.float32),
        in_specs=[pl.BlockSpec(memory_space=pl.ANY)] * 2,
        out_specs=pl.BlockSpec(memory_space=pltpu.VMEM),
        scratch_shapes=[
            pltpu.VMEM((4, 2 * ROWS, DEPTH), jnp.bfloat16),
            pltpu.VMEM((2, 4, COLS, DEPTH), jnp.bfloat16),
            pltpu.VMEM((BLOCKS, 8, ROWS, COLS), jnp.float32),
            pltpu.VMEM((BLOCKS, 2, 2, ROWS, COLS), jnp.float32),
            pltpu.VMEM((BLOCKS, 2, ROWS, COLS), jnp.float32),
            pltpu.VMEM((2, ROWS, COLS), jnp.float32),
            pltpu.VMEM((2, 2, 2, ROWS, COLS), jnp.float32),
            pltpu.VMEM((2, 2, ROWS, COLS), jnp.float32),
            pltpu.VMEM((ROWS, COLS), jnp.float32),
            dma((4, 2)), dma((4, 2)), dma((2,)), dma((2,)), dma((2,)), dma((2, 4)), dma((2, 4)), dma((2, 4)), dma((2, 4)),
            dma((BLOCKS, 2, 2)), dma((BLOCKS, 2, 2)), dma((BLOCKS, 2)), dma((BLOCKS, 2)),
            dma((2,)), dma((2,)), dma((2, 2, 2)), dma((2, 2, 2)), dma((2, 2)), dma((2, 2)), dma(()), dma(()),
        ],
        compiler_params=pltpu.CompilerParams(collective_id=0, has_side_effects=True, vmem_limit_bytes=60 << 20),
        name="ladder",
    )(amplitudes, pieces)
    return residual_in + ladder


def solution(mesh):
    return jax.shard_map(
        local,
        mesh=mesh,
        in_specs=(P("row", "col"), P(None, ("col", "row")), P("row", "col")),
        out_specs=P("row", "col"),
        check_vma=False,
    )
```

```python
import functools

import jax
import jax.numpy as jnp
from jax import lax
from jax.experimental import pallas as pl
from jax.experimental.pallas import tpu as pltpu
from jax.sharding import PartitionSpec as P

MESH = pl.DeviceIdType.MESH
ROWS = 48
COLS = 256
UNIT = 256
DEPTH = 4 * UNIT
BLOCKS = 8
OFFSETS = (2, 1, 3, 0)
TOP = (0, 4, 3, 6)
BOTTOM = (2, 1, 5, 7)

OUTER = (4, 3, 0, -1, -3, 2, -2, 1)
INNER = (4, 3, 0, -1, -3, -2, 2, 1)
OUTER_TURNS = (2, 4, 4, 8, 6, 7, 8, 9)
INNER_TURNS = (2, 4, 4, 9, 6, 7, 8, 9)
SCHEDULE = {
    "init": [("b", 0, 0), ("m", 0), ("a", 2, 0), ("a", 0, 1), ("b", 0, 1), ("a", 2, 1), ("b", 0, 2), ("b", 0, 3), ("b", 1, 0), ("a", 0, 2), ("a", 0, 3)],
    ("got", 0, 0): [("b", 1, 1), ("b", 1, 2), ("b", 1, 3)],
    ("got", 0, 3): [("m", 1), ("a", 2, 2)],
    ("got", 1, 0): [("a", 2, 3)],
}


def device(x, y, z, core):
    x, y, z = lax.rem(x + 4, 4), lax.rem(y + 4, 4), lax.rem(z + 8, 8)
    return (lax.rem(z, 4) * 8 + x * 2 + core, y * 2 + lax.div(z, 4))


def kernel(
    a_ref, b_ref, out_ref,
    a_all, b_all, part, near, far, z_first, z_ring, z_last, x_last,
    a_send, a_recv, b_local, mate_send, mate_recv, bx_send, bx_recv, fw_send, fw_recv,
    near_send, near_recv, far_send, far_recv, zf_send, zf_recv, zr_send, zr_recv, zl_send, zl_recv, xl_send, xl_recv,
):
    row, col = lax.axis_index("row"), lax.axis_index("col")
    core = lax.rem(row, 2)
    x = lax.rem(lax.div(row, 2), 4)
    z_low = lax.div(row, 8)
    y = lax.div(col, 2)
    z_high = lax.rem(col, 2)
    z = z_high * 4 + z_low
    mate = device(x, y, z, 1 - core)
    toward = 1 - 2 * core
    way = 1 - lax.rem(z_low, 2)
    sign = 1 - 2 * way
    outer = 1 - lax.rem(lax.div(z_low + 1, 2), 2)

    z_lows = (z_low, z_low + 1 - 2 * lax.rem(z_low, 2), 3 - z_low, lax.rem(z_low + 2, 4))

    barrier = pltpu.get_barrier_semaphore()
    partners = [mate, device(x + 1, y, z, core), device(x - 1, y, z, core)]
    partners += [device(x, y + 1, z, core), device(x, y - 1, z, core)]
    partners += [device(x + dx, y, z + dz, core) for dx in (0, 2) for dz in (1, -1)]
    partners += [device(x + dx, y, z_high * 4 + low, core) for low in z_lows for dx in (0, 2)][1:]
    for partner in partners:
        pl.semaphore_signal(barrier, inc=1, device_id=partner, device_id_type=MESH)

    def unit(start):
        return pl.ds(pl.multiple_of(start * UNIT, UNIT), UNIT)

    def a_pieces(dx, low):
        there = lax.rem(x + dx, 4)
        block = a_all.at[z_low, pl.ds(ROWS * (dx // 2), ROWS)]
        for units, slot, length in (
            (low * 8 + there * 2, 0, 2),
            (low * 8 + lax.rem(there + 3, 4) * 2, 2, 1),
            (low * 8 + lax.rem(there + 1, 4) * 2 + 1, 3, 1),
        ):
            source = a_ref.at[:, pl.ds(pl.multiple_of(units * UNIT, UNIT), length * UNIT)]
            yield source, block.at[:, slot * UNIT : (slot + length) * UNIT]

    def a_start(dx, turn):
        low = z_lows[turn]
        for source, target in a_pieces(dx, low):
            if dx == 0 and turn == 0:
                pltpu.make_async_copy(source, target, a_recv.at[0, 0]).start()
            else:
                pltpu.make_async_remote_copy(
                    source, target, a_send.at[turn, dx // 2], a_recv.at[turn, dx // 2],
                    device_id=device(x + dx, y, z_high * 4 + low, core), device_id_type=MESH,
                ).start()

    def a_copy(dx, turn):
        block = a_all.at[z_lows[turn], pl.ds(ROWS * (dx // 2), ROWS)]
        if dx == 0 and turn == 0:
            return pltpu.make_async_copy(block, block, a_recv.at[0, 0])
        return pltpu.make_async_remote_copy(
            block, block, a_send.at[turn, dx // 2], a_recv.at[turn, dx // 2], device_id=mate, device_id_type=MESH
        )

    def b_place(half, i):
        high = 1 - z_high if half == 0 else z_high
        return high, lax.rem(y + OFFSETS[i], 4)

    def b_across(half, i):
        high, ys = b_place(half, i)
        return pltpu.make_async_remote_copy(
            b_ref.at[ys, high], b_all.at[high, ys, :, unit(2 + core)], bx_send.at[half, i], bx_recv.at[half, i],
            device_id=device(x + toward, y, z, core), device_id_type=MESH,
        )

    def b_forward(half, i, slot):
        high, ys = b_place(half, i)
        here = b_all.at[high, ys, :, unit(slot)]
        return pltpu.make_async_remote_copy(
            here, here, fw_send.at[half, i], fw_recv.at[half, i], device_id=mate, device_id_type=MESH
        )

    def b_own(half):
        high = 1 - z_high if half == 0 else z_high
        return pltpu.make_async_copy(b_ref.at[:, high], b_all.at[high, :, :, unit(core)], b_local.at[half])

    def b_mate(half, slot):
        high = 1 - z_high if half == 0 else z_high
        return pltpu.make_async_remote_copy(
            b_ref.at[:, high], b_all.at[high, :, :, unit(slot)], mate_send.at[half], mate_recv.at[half],
            device_id=mate, device_id_type=MESH,
        )

    def run(when):
        for op in SCHEDULE.get(when, ()):
            if op[0] == "b":
                b_across(op[1], op[2]).start()
            elif op[0] == "m":
                b_mate(op[1], core).start()
            else:
                a_start(op[1], op[2])

    a_start(0, 0)
    b_own(0).start()
    b_own(1).start()
    pl.semaphore_wait(barrier, len(partners))
    run("init")

    steps = [sign * (step_out * outer + step_in * (1 - outer)) for step_out, step_in in zip(OUTER, INNER, strict=True)]

    def multiply(b, i):
        to = lax.rem(z + steps[b] + 8, 8)
        ys = lax.rem(y + OFFSETS[i], 4)
        product = lax.dot_general(
            a_all[lax.rem(to, 4)], b_all[lax.div(to, 4), ys], (((1,), (1,)), ((), ())), preferred_element_type=jnp.float32
        )
        part[b, TOP[i]] = product[:ROWS]
        part[b, BOTTOM[i]] = product[ROWS:]

    def near_copy(b, d, place):
        return pltpu.make_async_remote_copy(
            part.at[b, 2 * d + place], near.at[b, d, place], near_send.at[b, d, place], near_recv.at[b, d, place],
            device_id=device(x, y + 1 - 2 * d, z, core), device_id_type=MESH,
        )

    def far_copy(b, d):
        return pltpu.make_async_remote_copy(
            part.at[b, 4 + d], far.at[b, d], far_send.at[b, d], far_recv.at[b, d],
            device_id=device(x, y + 1 - 2 * d, z, core), device_id_type=MESH,
        )

    def z_first_copy(d):
        return pltpu.make_async_remote_copy(
            part.at[0, 6 + d], z_first.at[d], zf_send.at[d], zf_recv.at[d],
            device_id=device(x, y, z + 1 - 2 * d, core), device_id_type=MESH,
        )

    def z_ring_copy(b, d, step, half):
        return pltpu.make_async_remote_copy(
            part.at[b, 6 + half], z_ring.at[step, d, half], zr_send.at[step, d, half], zr_recv.at[step, d, half],
            device_id=device(x, y, z + 1 - 2 * d, core), device_id_type=MESH,
        )

    def z_last_copy(b, d, half):
        return pltpu.make_async_remote_copy(
            part.at[b, 6 + half], z_last.at[half, d], zl_send.at[half, d], zl_recv.at[half, d],
            device_id=device(x + 2 * half, y, z + 1 - 2 * d, core), device_id_type=MESH,
        )

    x_last_copy = pltpu.make_async_remote_copy(
        part.at[2, 7], x_last, xl_send, xl_recv, device_id=device(x + 2, y, z, core), device_id_type=MESH
    )

    def forward(half, i):
        b_across(half, i).wait_recv()
        b_forward(half, i, 2 + core).start()
        run(("got", half, i))

    def chunk(b, i):
        multiply(b, i)
        send(b, i)

    def send(b, i):
        if i == 0:
            near_copy(b, 0, 0).start()
            near_copy(b, 1, 0).start()
        elif i < 3:
            near_copy(b, i - 1, 1).start()

    def chunk2(b, c, i):
        to = lax.rem(z + steps[b] + 8, 8)
        other = lax.rem(z + steps[c] + 8, 8)
        both = jnp.concatenate([a_all[lax.rem(to, 4)], a_all[lax.rem(other, 4)]], axis=0)
        product = lax.dot_general(
            both, b_all[lax.div(to, 4), lax.rem(y + OFFSETS[i], 4)], (((1,), (1,)), ((), ())), preferred_element_type=jnp.float32
        )
        for place, block in enumerate((b, c)):
            part[block, TOP[i]] = product[2 * place * ROWS : (2 * place + 1) * ROWS]
            part[block, BOTTOM[i]] = product[(2 * place + 1) * ROWS : (2 * place + 2) * ROWS]
            send(block, i)

    def got_a(turn):
        if turn:
            a_copy(0, turn).wait_recv()
        else:
            a_copy(0, 0).wait()
        a_copy(2, turn).wait_recv()

    def got_b(half, i):
        if i == 0:
            b_own(half).wait()
            b_mate(half, 1 - core).wait_recv()
        forward(half, i)
        b_forward(half, i, 3 - core).wait_recv()

    def begin(b):
        for i in range(4):
            chunk(b, i)

    def pass_on(b):
        for d in range(2):
            near_copy(b, d, 0).wait_recv()
            part[b, 4 + d] += near[b, d, 0]
            far_copy(b, d).start()

    def finish(b):
        for d in range(2):
            far_copy(b, d).wait_recv()
            near_copy(b, d, 1).wait_recv()
        part[b, 6] += far[b, 0] + near[b, 1, 1]
        part[b, 7] += far[b, 1] + near[b, 0, 1]
    def along_z(b, step):
        d = way if step > 0 else 1 - way
        if step == 4:
            z_first_copy(0).start()
            z_first_copy(1).start()
        elif abs(step) == 3:
            z_ring_copy(b, d, 0, 1 - d).start()
            z_first_copy(d).wait_recv()
            part[b, 6 + d] += z_first[d]
            z_ring_copy(b, d, 0, d).start()
        elif step:
            for half in (1, 0):
                z_ring_copy(b, d, 2 - abs(step), half).wait_recv()
                part[b, 6 + half] += z_ring[2 - abs(step), d, half]
                if abs(step) == 2:
                    z_ring_copy(b, d, 1, half).start()
                else:
                    z_last_copy(b, d, half).start()
        else:
            x_last_copy.start()

    def move(t, steps, turns):
        for b in sorted(range(BLOCKS), key=lambda b: (-abs(steps[b]), b)):
            if turns[b] == t:
                along_z(b, steps[b])

    def settle(b):
        if b < BLOCKS:
            finish(b)
        pl.when(outer == 1)(functools.partial(move, b + 2, OUTER, OUTER_TURNS))
        pl.when(outer == 0)(functools.partial(move, b + 2, INNER, INNER_TURNS))

    got_a(0)
    got_b(0, 0)
    chunk(0, 0)
    got_b(0, 1)
    chunk(0, 1)
    got_a(1)
    chunk(1, 0)
    chunk(1, 1)
    got_b(0, 2)
    chunk(0, 2)
    chunk(1, 2)
    pass_on(0)
    got_b(0, 3)
    chunk(0, 3)
    chunk(1, 3)
    pass_on(1)
    for i in range(4):
        got_b(1, i)
        chunk2(2, 3, i)
        if i == 1:
            settle(0)
        if i == 2:
            settle(1)
            pass_on(2)
    pass_on(3)
    got_a(2)
    begin(4)
    got_a(3)
    begin(5)
    settle(2)
    pass_on(4)
    begin(6)
    settle(3)
    pass_on(5)
    begin(7)
    settle(4)
    pass_on(6)
    settle(5)
    pass_on(7)
    settle(6)
    settle(7)

    for half in range(2):
        for d in range(2):
            z_last_copy(5, d, half).wait_recv()
    x_last_copy.wait_recv()
    out_ref[...] = part[2, 6] + x_last[...] + z_last[0, 0] + z_last[0, 1] + z_last[1, 0] + z_last[1, 1]

    for turn in range(4):
        for dx in (0, 2):
            if turn or dx:
                a_copy(dx, turn).wait_send()
    for half in range(2):
        b_mate(half, core).wait_send()
        for i in range(4):
            b_across(half, i).wait_send()
            b_forward(half, i, 2 + core).wait_send()
    for b in range(BLOCKS):
        for d in range(2):
            near_copy(b, d, 0).wait_send()
            near_copy(b, d, 1).wait_send()
            far_copy(b, d).wait_send()
    for d in range(2):
        z_first_copy(d).wait_send()
        for step in range(2):
            for half in range(2):
                z_ring_copy(1, d, step, half).wait_send()
        for half in range(2):
            z_last_copy(5, d, half).wait_send()
    x_last_copy.wait_send()


def local(amplitudes, integrals, residual_in):
    pieces = integrals.reshape(4, 2, COLS, UNIT)
    dma = pltpu.SemaphoreType.DMA
    ladder = pl.pallas_call(
        kernel,
        out_shape=jax.ShapeDtypeStruct((ROWS, COLS), jnp.float32),
        in_specs=[pl.BlockSpec(memory_space=pl.ANY)] * 2,
        out_specs=pl.BlockSpec(memory_space=pltpu.VMEM),
        scratch_shapes=[
            pltpu.VMEM((4, 2 * ROWS, DEPTH), jnp.bfloat16),
            pltpu.VMEM((2, 4, COLS, DEPTH), jnp.bfloat16),
            pltpu.VMEM((BLOCKS, 8, ROWS, COLS), jnp.float32),
            pltpu.VMEM((BLOCKS, 2, 2, ROWS, COLS), jnp.float32),
            pltpu.VMEM((BLOCKS, 2, ROWS, COLS), jnp.float32),
            pltpu.VMEM((2, ROWS, COLS), jnp.float32),
            pltpu.VMEM((2, 2, 2, ROWS, COLS), jnp.float32),
            pltpu.VMEM((2, 2, ROWS, COLS), jnp.float32),
            pltpu.VMEM((ROWS, COLS), jnp.float32),
            dma((4, 2)), dma((4, 2)), dma((2,)), dma((2,)), dma((2,)), dma((2, 4)), dma((2, 4)), dma((2, 4)), dma((2, 4)),
            dma((BLOCKS, 2, 2)), dma((BLOCKS, 2, 2)), dma((BLOCKS, 2)), dma((BLOCKS, 2)),
            dma((2,)), dma((2,)), dma((2, 2, 2)), dma((2, 2, 2)), dma((2, 2)), dma((2, 2)), dma(()), dma(()),
        ],
        compiler_params=pltpu.CompilerParams(collective_id=0, has_side_effects=True, vmem_limit_bytes=60 << 20),
        name="ladder",
    )(amplitudes, pieces)
    return residual_in + ladder


def solution(mesh):
    return jax.shard_map(
        local,
        mesh=mesh,
        in_specs=(P("row", "col"), P(None, ("col", "row")), P("row", "col")),
        out_specs=P("row", "col"),
        check_vma=False,
    )
```
